32 devices in a mesh: grp: 2 (over y), mesh: 4 (over z), col: 2 (over x), term: 2 (over core).
Axes of the slice: x: 2, y: 2, z: 4, core: 2. Of those that a mesh axis runs over, the one named last changes fastest.
Arguments:
- basis: bfloat16 [4096, 512], P(('grp', 'mesh'), 'col'), parts along dimension 0, may hold values from -2 to 2
- blocks: bfloat16 [2, 32, 20, 128, 128], P('term', ('grp', 'mesh', 'col')), parts along dimension 1, may hold values from -0.125 to 0.125
- col_index: int32 [2, 32, 20], P('term', ('grp', 'mesh', 'col')), parts along dimension 1, may hold values from 0 to 5, as said below
- send_rows: int32 [8, 2, 1], P(('grp', 'mesh')), parts along dimension 0, may hold values from 0 to 3, as said below
- part_rows: int32 [8], P(('grp', 'mesh')), parts along dimension 0, may hold values from 1 to 4, as said below
Outputs:
- reduced: float32 [2, 1024, 512], P('term', ('grp', 'mesh', 'col')), parts along dimension 1
The draws below stay inside these ranges and needn't reach their ends.
There are 2 independent parts, one for each index of `grp`. The reference program is written for one: setup_inputs(seed, part) draws one part's arguments, and reference() takes and returns one part's arrays. A program takes and returns all parts, laid end to end along the dimension named above; each array names one. Nothing has to cross between parts.
Inputs may be any that keep to these rules, and one draw needn't show every extreme that they name: `part_rows`: some partition has all 4 block rows live. `send_rows`: every entry is a live block row of the sending partition p; [p, 0, :] go to partition p - 1, [p, 1, :] to partition p + 1. `col_index`: slots 0 to 0 are the rows received from the lower partition, 1 to 4 the partition's own block rows in order, the last 1 those from the upper partition. Entry k = 0 is the block row's own slot; other entries may repeat.
All inputs are finite; a program needn't handle non-finite values.
Results may differ from the reference program's by a relative error of at most 0.0029.
Values may be sent and summed in bfloat16 or wider, within the bound.
A program may use at most 64 MiB of HBM per device.

```python
import jax
import jax.numpy as jnp
from jax import lax

BS = 128
R = 512
NNZ = 20
TERMS = 2
NB = 4
HB = 1
NBT = 16
NDOF = 2048


def shared_rows(key):
    first, second, third = jax.random.split(jax.random.fold_in(key, 7), 3)
    partitions = NBT // NB
    live = jax.random.randint(first, (partitions,), HB, NB + 1)
    fullest = jax.random.randint(second, (), 0, partitions)
    live = live.at[fullest].set(NB)
    raw = jax.random.randint(third, (partitions, 2, HB), 0, 1 << 20)
    sends = raw % live[:, None, None]
    sends = sends.at[:, 0, 0].set(0)
    sends = sends.at[fullest, 1, 0].set(NB - 1)
    return (live.astype(jnp.int32), sends.astype(jnp.int32))


def draw_part_rows(key, part):
    return shared_rows(key)[0]


def draw_send_rows(key, part):
    return shared_rows(key)[1]


def draw_col_index(key, part):
    others = jax.random.randint(jax.random.fold_in(key, 11), (TERMS, NBT, NNZ), 0, NB + 2 * HB)
    own_slot = HB + jnp.arange(NBT) % NB
    slots = others.at[:, :, 0].set(own_slot[None, :])
    slots = slots.at[:, 0, 1].set(0)
    slots = slots.at[:, NBT - 1, 1].set(NB + 2 * HB - 1)
    return slots.astype(jnp.int32)


def shard_levels(stream_key, dims, cuts, smallest, high):
    level = 1.0
    for position, parts in cuts:
        heights = jax.random.uniform(jax.random.fold_in(jax.random.fold_in(stream_key, 6), position), (parts,), jnp.float32, smallest / len(cuts), high / len(cuts))
        level = level * jnp.repeat(jnp.exp(heights), dims[position] // parts).reshape((-1,) + (1,) * (len(dims) - 1 - position))
    return level


def bell_draw(stream_key, extent, scale, limit, cuts=(), kind=jnp.bfloat16):
    gain = shard_levels(stream_key, extent, cuts, -0.22, 0.18) if cuts else 1.0
    drawn = jax.random.normal(stream_key, extent, jnp.float32) * scale * gain
    return jnp.minimum(jnp.maximum(drawn, -limit), limit).astype(kind)


def setup_inputs(seed: int = 0, part: int = 0) -> dict:
    streams_of = jax.random.split(jax.random.key(seed), 6)
    part_keys = jax.random.split(jax.random.fold_in(streams_of[5], part), 6)
    return {
        "basis": bell_draw(part_keys[0], (NDOF, R), (NDOF ** -0.25), 2.0, ((0, 4), (1, 2))),
        "blocks": bell_draw(part_keys[1], (TERMS, NBT, NNZ, BS, BS), (NNZ * BS) ** -0.5, 0.125, ((0, 2), (1, 8))),
        "col_index": draw_col_index(jax.random.fold_in(jax.random.fold_in(streams_of[5], part), 71), part),
        "send_rows": draw_send_rows(jax.random.fold_in(jax.random.fold_in(streams_of[5], part), 71), part),
        "part_rows": draw_part_rows(jax.random.fold_in(jax.random.fold_in(streams_of[5], part), 71), part),
    }


def reference(basis, blocks, col_index, send_rows, part_rows):
    partitions = NBT // NB
    basis_rows = basis.reshape(partitions, NB, BS, R)
    live = jnp.arange(NB)[None, :] < part_rows[:, None]
    basis_rows = jnp.where(live[:, :, None, None], basis_rows, jnp.zeros((), jnp.bfloat16))
    sent = basis_rows[jnp.arange(partitions)[:, None, None], send_rows]
    blank = jnp.zeros((1, HB, BS, R), jnp.bfloat16)
    from_lower = jnp.concatenate([blank, sent[:-1, 1]], axis=0)
    from_upper = jnp.concatenate([sent[1:, 0], blank], axis=0)
    extended = jnp.concatenate([from_lower, basis_rows, from_upper], axis=1)
    term_blocks = blocks.reshape(TERMS, partitions, NB, NNZ, BS, BS)
    slot_index = col_index.reshape(TERMS, partitions, NB, NNZ)
    results = []
    for q in range(TERMS):
        def step(totals, element):
            kq, cq, ext_rows, own_rows = element

            def accumulate(k, running):
                picked = jnp.take(ext_rows, cq[:, k], axis=0)
                return running + jnp.einsum('bij,bjc->bic', kq[:, k].astype(jnp.float32), picked.astype(jnp.float32))

            product = lax.fori_loop(0, NNZ, accumulate, jnp.zeros((NB, BS, R), jnp.float32))
            rounded = product.astype(jnp.bfloat16).reshape(NB * BS, R)
            flat_rows = own_rows.reshape(NB * BS, R)
            gram = lax.dot_general(flat_rows, rounded, (((0,), (0,)), ((), ())), preferred_element_type=jnp.float32)
            return totals + gram, None

        totals, unused = lax.scan(step, jnp.zeros((R, R), jnp.float32), (term_blocks[q], slot_index[q], extended, basis_rows))
        results.append(totals)
    return jnp.stack(results)
```

```python
import functools

import jax
import jax.numpy as jnp
from jax import lax
from jax.experimental import pallas as pl
from jax.experimental.pallas import tpu as pltpu
from jax.sharding import PartitionSpec as P

BS = 128
MESH = pl.DeviceIdType.MESH


def from_behind(x, axis, by):
    length = lax.axis_size(axis)
    pairs = [(i, i + by) for i in range(length) if 0 <= i + by < length]
    return lax.ppermute(x, axis, pairs)


def general(basis, blocks, col_index, send_rows, part_rows):
    panel_width = basis.shape[1]
    local_blocks = basis.shape[0] // BS
    halo_count = send_rows.shape[2]
    device_blocks = blocks.shape[1]
    stored = blocks.shape[2]
    live = jnp.arange(local_blocks) < part_rows[0]
    panel = jnp.where(
        live[:, None, None],
        basis.reshape(local_blocks, BS, panel_width),
        jnp.zeros((), jnp.bfloat16),
    )
    going_down = jnp.take(panel, send_rows[0, 0], axis=0)
    going_up = jnp.take(panel, send_rows[0, 1], axis=0)
    from_lower = from_behind(going_up, "mesh", 1)
    from_upper = from_behind(going_down, "mesh", -1)
    ext_panel = jnp.concatenate([from_lower, panel, from_upper], axis=0)
    extended = lax.all_gather(ext_panel, "col", axis=2, tiled=True)
    full_width = extended.shape[2]
    term_blocks = blocks[0]
    slot_index = col_index[0]

    def accumulate(k, running):
        picked = jnp.take(extended, slot_index[:, k], axis=0)
        return running + jnp.einsum(
            "bij,bjc->bic", term_blocks[:, k], picked, preferred_element_type=jnp.float32
        )

    product = lax.fori_loop(
        0, stored, accumulate, jnp.zeros((device_blocks, BS, full_width), jnp.float32)
    )
    rounded = product.astype(jnp.bfloat16).reshape(device_blocks * BS, full_width)
    first_block = halo_count + lax.axis_index("col") * device_blocks
    own_rows = lax.dynamic_slice_in_dim(extended, first_block, device_blocks, 0).reshape(
        device_blocks * BS, full_width
    )
    reduced = lax.psum_scatter(
        lax.dot_general(
            own_rows, rounded, (((0,), (0,)), ((), ())), preferred_element_type=jnp.float32
        ),
        ("mesh", "col"),
        scatter_dimension=0,
        tiled=True,
    )
    return reduced[None]


def kernel(
    parts,
    cores,
    part_ref,
    send_ref,
    col_ref,
    basis_ref,
    blocks_ref,
    out_ref,
    basis_v,
    blocks_v,
    other_raw,
    ext_own,
    ext_other,
    stage,
    p_send,
    p_all,
    g32,
    g_send,
    g_recv,
    local_sem,
    x_send,
    x_recv,
    z_send,
    z_recv,
    g_ssem,
    g_rsem,
):
    g = lax.axis_index("grp")
    m = lax.axis_index("mesh")
    c = lax.axis_index("col")
    t = lax.axis_index("term")
    lb, _, width = basis_v.shape
    halo = send_ref.shape[1]
    rows, stored = blocks_v.shape[:2]
    ranks = 2 * parts
    rank = 2 * m + c
    half = lb // cores
    piece = g_send.shape[0] // ranks
    mine = (g, m, 1 - c, t)
    sibling = (g, m, c, 1 - t)

    load_basis = pltpu.make_async_copy(basis_ref, basis_v, local_sem.at[0])
    load_basis.start()
    load_blocks = pltpu.make_async_copy(blocks_ref, blocks_v, local_sem.at[1])
    load_blocks.start()

    def peer(d):
        r = lax.rem(rank + d, ranks)
        return (g, r // 2, lax.rem(r, 2), t), r

    barrier = pltpu.get_barrier_semaphore()
    for d in range(1, ranks):
        pl.semaphore_signal(barrier, inc=1, device_id=peer(d)[0], device_id_type=MESH)
    pl.semaphore_signal(barrier, inc=1, device_id=sibling, device_id_type=MESH)
    pl.semaphore_wait(barrier, ranks)

    def remote(src, dst, ssem, rsem, to):
        return pltpu.make_async_remote_copy(
            src_ref=src, dst_ref=dst, send_sem=ssem, recv_sem=rsem, device_id=to, device_id_type=MESH
        )

    span = pl.ds(t * half, half)
    across = remote(basis_ref.at[span], other_raw.at[span], x_send.at[0], x_recv.at[0], mine)
    across.start()

    load_basis.wait()
    low = pl.ds(0, halo)
    high = pl.ds(lb + halo, halo)

    def halo_copies(ext, base):
        up = remote(stage.at[base], ext.at[low], z_send.at[base], z_recv.at[base], (g, lax.rem(m + 1, parts), c, t))
        down = remote(
            stage.at[base + 1],
            ext.at[high],
            z_send.at[base + 1],
            z_recv.at[base + 1],
            (g, lax.rem(m + parts - 1, parts), c, t),
        )
        return up, down

    def send_halo(raw, ext, base):
        for j in range(halo):
            stage[base, j] = raw[send_ref[1, j]]
            stage[base + 1, j] = raw[send_ref[0, j]]
        up, down = halo_copies(ext, base)

        @pl.when(m < parts - 1)
        def _():
            up.start()

        @pl.when(m > 0)
        def _():
            down.start()

        @pl.when(m == 0)
        def _():
            ext[low] = jnp.zeros((halo, BS, width), jnp.bfloat16)

        @pl.when(m == parts - 1)
        def _():
            ext[high] = jnp.zeros((halo, BS, width), jnp.bfloat16)

        for i in range(lb):
            ext[halo + i] = jnp.where(i < part_ref[0], raw[i], jnp.zeros((), jnp.bfloat16))

    def wait_halo(ext, base):
        up, down = halo_copies(ext, base)

        @pl.when(m > 0)
        def _():
            up.wait_recv()

        @pl.when(m < parts - 1)
        def _():
            down.wait_recv()

    def drain_halo(ext, base):
        up, down = halo_copies(ext, base)

        @pl.when(m < parts - 1)
        def _():
            up.wait_send()

        @pl.when(m > 0)
        def _():
            down.wait_send()

    def product(ext, r):
        total = jnp.zeros((BS, width), jnp.float32)
        step = 2 if stored % 2 == 0 else 1
        for k in range(0, stored, step):
            left = jnp.concatenate([blocks_v[r, k + j] for j in range(step)], axis=1)
            right = jnp.concatenate([ext[col_ref[r, k + j]] for j in range(step)], axis=0)
            total = total + jnp.dot(left, right, preferred_element_type=jnp.float32)
        return total.astype(jnp.bfloat16)

    send_halo(basis_v, ext_own, 0)
    load_blocks.wait()
    wait_halo(ext_own, 0)
    for r in range(rows):
        p_send[pl.ds(r * BS, BS)] = product(ext_own, r)
    swap = remote(p_send, p_all.at[pl.ds(c * rows * BS, rows * BS)], x_send.at[1], x_recv.at[1], mine)
    swap.start()

    across.wait_recv()
    inner = remote(other_raw.at[span], other_raw.at[span], x_send.at[2], x_recv.at[2], sibling)
    inner.start()
    inner.wait_recv()
    send_halo(other_raw, ext_other, 2)
    wait_halo(ext_other, 2)
    for r in range(rows):
        p_all[pl.ds(c * rows * BS + r * BS, BS)] = product(ext_other, r)
    swap.wait_recv()

    right = p_all[...]

    def gram(ext):
        left = ext[pl.ds(halo, lb)].reshape(lb * BS, width)
        return lax.dot_general(left, right, (((0,), (0,)), ((), ())), preferred_element_type=jnp.float32)

    for ext, where in ((ext_own, c), (ext_other, 1 - c)):
        value = gram(ext)
        g32[pl.ds(where * width, width)] = value
        g_send[pl.ds(where * width, width)] = value.astype(jnp.bfloat16)

    def share(d):
        to, r = peer(d)
        return remote(g_send.at[pl.ds(r * piece, piece)], g_recv.at[d - 1], g_ssem.at[d - 1], g_rsem.at[d - 1], to)

    for d in range(1, ranks):
        share(d).start()

    same = g32[pl.ds(rank * piece, piece)]
    crossed = jnp.zeros_like(same)
    for d in range(1, ranks):
        share(d).wait_recv()
        if d % 2:
            crossed = crossed + g_recv[d - 1].astype(jnp.float32)
        else:
            same = same + g_recv[d - 1].astype(jnp.float32)
    out_ref[:, pl.ds(pl.multiple_of((1 - c) * width, width), width)] = same
    out_ref[:, pl.ds(pl.multiple_of(c * width, width), width)] = crossed

    across.wait_send()
    swap.wait_send()
    inner.wait_send()
    drain_halo(ext_own, 0)
    drain_halo(ext_other, 2)
    for d in range(1, ranks):
        share(d).wait_send()


def fused(parts, cores, basis, blocks, col_index, send_rows, part_rows):
    width = basis.shape[1]
    lb = basis.shape[0] // BS
    halo = send_rows.shape[2]
    rows, stored = blocks.shape[1:3]
    full = 2 * width
    ranks = 2 * parts
    piece = full // ranks
    bf16 = jnp.bfloat16
    smem = pl.BlockSpec(memory_space=pltpu.SMEM)
    hbm = pl.BlockSpec(memory_space=pl.ANY)
    reduced = pl.pallas_call(
        functools.partial(kernel, parts, cores),
        out_shape=jax.ShapeDtypeStruct((piece, full), jnp.float32),
        in_specs=[smem, smem, smem, hbm, hbm],
        out_specs=pl.BlockSpec(memory_space=pltpu.VMEM),
        scratch_shapes=[
            pltpu.VMEM((lb, BS, width), bf16),
            pltpu.VMEM((rows, stored, BS, BS), bf16),
            pltpu.VMEM((lb, BS, width), bf16),
            pltpu.VMEM((lb + 2 * halo, BS, width), bf16),
            pltpu.VMEM((lb + 2 * halo, BS, width), bf16),
            pltpu.VMEM((4, halo, BS, width), bf16),
            pltpu.VMEM((rows * BS, width), bf16),
            pltpu.VMEM((lb * BS, width), bf16),
            pltpu.VMEM((full, width), jnp.float32),
            pltpu.VMEM((full, width), bf16),
            pltpu.VMEM((ranks - 1, piece, width), bf16),
            pltpu.SemaphoreType.DMA((2,)),
            pltpu.SemaphoreType.DMA((3,)),
            pltpu.SemaphoreType.DMA((3,)),
            pltpu.SemaphoreType.DMA((4,)),
            pltpu.SemaphoreType.DMA((4,)),
            pltpu.SemaphoreType.DMA((ranks - 1,)),
            pltpu.SemaphoreType.DMA((ranks - 1,)),
        ],
        compiler_params=pltpu.CompilerParams(
            collective_id=0, has_side_effects=True, vmem_limit_bytes=24 * 1024 * 1024
        ),
    )(part_rows, send_rows[0], col_index[0], basis.reshape(lb, BS, width), blocks[0])
    return reduced[None]


def solution(mesh):
    placed = (
        P(("grp", "mesh"), "col"),
        P("term", ("grp", "mesh", "col"), None, None, None),
        P("term", ("grp", "mesh", "col"), None),
        P(("grp", "mesh"), None, None),
        P(("grp", "mesh")),
    )
    parts, cols, cores = mesh.shape["mesh"], mesh.shape["col"], mesh.shape["term"]

    def local(basis, blocks, col_index, send_rows, part_rows):
        lb = basis.shape[0] // BS
        fits = (
            cols == 2
            and cores == 2
            and basis.shape[1] % BS == 0
            and lb % cores == 0
            and lb == 2 * blocks.shape[1]
            and (2 * basis.shape[1]) % (2 * parts * 16) == 0
        )
        if fits:
            return fused(parts, cores, basis, blocks, col_index, send_rows, part_rows)
        return general(basis, blocks, col_index, send_rows, part_rows)

    return jax.shard_map(
        local,
        mesh=mesh,
        in_specs=placed,
        out_specs=P("term", ("grp", "mesh", "col"), None),
        check_vma=False,
    )
```

```python
import functools

import jax
import jax.numpy as jnp
from jax import lax
from jax.experimental import pallas as pl
from jax.experimental.pallas import tpu as pltpu
from jax.sharding import PartitionSpec as P

BS = 128
MESH = pl.DeviceIdType.MESH


def from_behind(x, axis, by):
    length = lax.axis_size(axis)
    pairs = [(i, i + by) for i in range(length) if 0 <= i + by < length]
    return lax.ppermute(x, axis, pairs)


def general(basis, blocks, col_index, send_rows, part_rows):
    panel_width = basis.shape[1]
    local_blocks = basis.shape[0] // BS
    halo_count = send_rows.shape[2]
    device_blocks = blocks.shape[1]
    stored = blocks.shape[2]
    live = jnp.arange(local_blocks) < part_rows[0]
    panel = jnp.where(
        live[:, None, None],
        basis.reshape(local_blocks, BS, panel_width),
        jnp.zeros((), jnp.bfloat16),
    )
    going_down = jnp.take(panel, send_rows[0, 0], axis=0)
    going_up = jnp.take(panel, send_rows[0, 1], axis=0)
    from_lower = from_behind(going_up, "mesh", 1)
    from_upper = from_behind(going_down, "mesh", -1)
    ext_panel = jnp.concatenate([from_lower, panel, from_upper], axis=0)
    extended = lax.all_gather(ext_panel, "col", axis=2, tiled=True)
    full_width = extended.shape[2]
    term_blocks = blocks[0]
    slot_index = col_index[0]

    def accumulate(k, running):
        picked = jnp.take(extended, slot_index[:, k], axis=0)
        return running + jnp.einsum(
            "bij,bjc->bic", term_blocks[:, k], picked, preferred_element_type=jnp.float32
        )

    product = lax.fori_loop(
        0, stored, accumulate, jnp.zeros((device_blocks, BS, full_width), jnp.float32)
    )
    rounded = product.astype(jnp.bfloat16).reshape(device_blocks * BS, full_width)
    first_block = halo_count + lax.axis_index("col") * device_blocks
    own_rows = lax.dynamic_slice_in_dim(extended, first_block, device_blocks, 0).reshape(
        device_blocks * BS, full_width
    )
    reduced = lax.psum_scatter(
        lax.dot_general(
            own_rows, rounded, (((0,), (0,)), ((), ())), preferred_element_type=jnp.float32
        ),
        ("mesh", "col"),
        scatter_dimension=0,
        tiled=True,
    )
    return reduced[None]


def kernel(
    parts,
    cores,
    part_hbm,
    send_hbm,
    col_hbm,
    basis_ref,
    blocks_ref,
    out_ref,
    part_ref,
    send_ref,
    col_ref,
    basis_v,
    blocks_v,
    other_raw,
    ext_own,
    ext_other,
    stage,
    turned,
    p_send,
    p_all,
    g32,
    g_send,
    g_recv,
    local_sem,
    x_send,
    x_recv,
    z_send,
    z_recv,
    g_ssem,
    g_rsem,
    ok_sem,
):
    g = lax.axis_index("grp")
    m = lax.axis_index("mesh")
    c = lax.axis_index("col")
    t = lax.axis_index("term")
    strips, lb = basis_v.shape[:2]
    width = strips * BS
    halo = send_ref.shape[0]
    rows, stored = blocks_v.shape[:2]
    ranks = 2 * parts
    rank = 2 * m + c
    half = lb // cores
    piece = g_send.shape[1] // ranks
    opposite = (g, m, 1 - c, t)
    sibling = (g, m, c, 1 - t)
    below = lax.rem(m + parts - 1, parts)
    above = lax.rem(m + 1, parts)
    has_lower = m > 0
    has_upper = m < parts - 1
    everyone = range(strips)

    def strip(q):
        return pl.ds(q * BS, BS)

    load_basis = [
        pltpu.make_async_copy(basis_ref.at[:, :, strip(q)], basis_v.at[q], local_sem.at[4 + q]) for q in everyone
    ]
    load_small = [
        pltpu.make_async_copy(hbm, ref, local_sem.at[1 + n])
        for n, (hbm, ref) in enumerate(((send_hbm, send_ref), (part_hbm, part_ref), (col_hbm, col_ref)))
    ]
    load_blocks = pltpu.make_async_copy(blocks_ref, blocks_v, local_sem.at[0])
    for load in load_basis + load_small + [load_blocks]:
        load.start()

    def peer(d):
        r = lax.rem(rank + d, ranks)
        return (g, r // 2, lax.rem(r, 2), t), r

    for load in load_basis + load_small:
        load.wait()
    for j in range(halo):
        for q in everyone:
            stage[0, q, j] = basis_v[q, send_ref[j, 1]]
            stage[1, q, j] = basis_v[q, send_ref[j, 0]]

    barrier = pltpu.get_barrier_semaphore()
    for to in (sibling, opposite):
        pl.semaphore_signal(barrier, inc=1, device_id=to, device_id_type=MESH)
    for there, z in ((has_lower, below), (has_upper, above)):

        @pl.when(there)
        def _():
            for side in (c, 1 - c):
                pl.semaphore_signal(barrier, inc=1, device_id=(g, z, side, t), device_id_type=MESH)

    sides = has_lower.astype(jnp.int32) + has_upper.astype(jnp.int32)
    pl.semaphore_wait(barrier, 2 + 2 * sides)

    def remote(src, dst, ssem, rsem, to):
        return pltpu.make_async_remote_copy(
            src_ref=src, dst_ref=dst, send_sem=ssem, recv_sem=rsem, device_id=to, device_id_type=MESH
        )

    span = pl.ds(t * half, half)
    edge = pl.ds(t * (lb + halo), halo)
    ahead, behind = m + 1 - 2 * t, m - 1 + 2 * t
    has_ahead = jnp.logical_and(ahead >= 0, ahead < parts)
    has_behind = jnp.logical_and(behind >= 0, behind < parts)
    forward = lax.rem(ahead + parts, parts)
    across = remote(basis_v.at[:, span], other_raw.at[:, span], x_send.at[0], x_recv.at[0], opposite)
    inner = remote(other_raw.at[:, span], other_raw.at[:, span], x_send.at[1], x_recv.at[1], sibling)
    slant = remote(stage.at[t], ext_other.at[:, edge], x_send.at[2], x_recv.at[2], (g, forward, 1 - c, t))
    inner_edge = remote(ext_other.at[:, edge], ext_other.at[:, edge], x_send.at[3], x_recv.at[3], sibling)
    placed = pl.ds(c * rows * BS, rows * BS)
    swap = [remote(p_send.at[q], p_all.at[q, placed], x_send.at[4 + q], x_recv.at[4 + q], opposite) for q in everyone]
    low = pl.ds(0, halo)
    high = pl.ds(lb + halo, halo)
    up = remote(stage.at[0], ext_own.at[:, low], z_send.at[0], z_recv.at[0], (g, above, c, t))
    down = remote(stage.at[1], ext_own.at[:, high], z_send.at[1], z_recv.at[1], (g, below, c, t))

    across.start()
    pl.when(has_upper)(up.start)
    pl.when(has_lower)(down.start)
    pl.when(has_ahead)(slant.start)

    def fill(raw, ext):
        for q in everyone:
            for i in range(lb):
                ext[q, halo + i] = jnp.where(i < part_ref[0], raw[q, i], jnp.zeros((), jnp.bfloat16))

    blank = jnp.zeros((strips, halo, BS, BS), jnp.bfloat16)
    for there, where in ((has_lower, low), (has_upper, high)):

        @pl.when(jnp.logical_not(there))
        def _():
            ext_own[:, where] = blank
            ext_other[:, where] = blank

    def product(ext, r):
        total = jnp.zeros((BS, width), jnp.float32)
        step = 2 if stored % 2 == 0 else 1
        for k in range(0, stored, step):
            left = jnp.concatenate([blocks_v[r, k + j] for j in range(step)], axis=1)
            right = jnp.concatenate(
                [
                    jnp.concatenate([ext[q, col_ref[r, k + j]] for q in everyone], axis=1)
                    for j in range(step)
                ],
                axis=0,
            )
            total = total + jnp.dot(left, right, preferred_element_type=jnp.float32)
        return total.astype(jnp.bfloat16)

    def turn(ext, where):
        for q in everyone:
            body = ext[q, pl.ds(halo, lb)].reshape(lb * BS, BS)
            turned[pl.ds(where * width + q * BS, BS)] = body.T

    def share(d, q):
        to, r = peer(d)
        return remote(
            g_send.at[q, pl.ds(r * piece, piece)],
            g_recv.at[q, d - 1],
            g_ssem.at[q, d - 1],
            g_rsem.at[q, d - 1],
            to,
        )

    order = sorted(range(1, ranks), key=lambda d: abs(d - parts))

    fill(basis_v, ext_own)
    load_blocks.wait()
    pl.when(has_lower)(up.wait_recv)
    pl.when(has_upper)(down.wait_recv)
    for there, z in ((has_lower, below), (has_upper, above)):

        @pl.when(there)
        def _():
            pl.semaphore_signal(ok_sem, inc=1, device_id=(g, z, c, t), device_id_type=MESH)

    for r in range(rows):
        value = product(ext_own, r)
        for q in everyone:
            p_send[q, pl.ds(r * BS, BS)] = value[:, q * BS : (q + 1) * BS]
    for q in everyone:
        swap[q].start()
    across.wait_recv()
    inner.start()

    @pl.when(has_behind)
    def _():
        slant.wait_recv()
        inner_edge.start()

    turn(ext_own, c)
    inner.wait_recv()
    fill(other_raw, ext_other)
    turn(ext_other, 1 - c)
    pl.when(has_ahead)(inner_edge.wait_recv)
    for r in range(rows):
        value = product(ext_other, r)
        for q in everyone:
            p_all[q, pl.ds(c * rows * BS + r * BS, BS)] = value[:, q * BS : (q + 1) * BS]
    pl.semaphore_wait(ok_sem, sides)

    for q in everyone:
        swap[q].wait_recv()
        value = jnp.dot(turned[...], p_all[q], preferred_element_type=jnp.float32)
        g32[q] = value
        g_send[q] = value.astype(jnp.bfloat16)
        for d in order:
            share(d, q).start()

    for q in everyone:
        same = g32[q, pl.ds(rank * piece, piece)]
        crossed = jnp.zeros_like(same)
        for d in reversed(order):
            share(d, q).wait_recv()
            if d % 2:
                crossed = crossed + g_recv[q, d - 1].astype(jnp.float32)
            else:
                same = same + g_recv[q, d - 1].astype(jnp.float32)
        out_ref[:, pl.ds(pl.multiple_of((1 - c) * width + q * BS, BS), BS)] = same
        out_ref[:, pl.ds(pl.multiple_of(c * width + q * BS, BS), BS)] = crossed

    across.wait_send()
    inner.wait_send()
    pl.when(has_ahead)(slant.wait_send)
    pl.when(has_behind)(inner_edge.wait_send)
    pl.when(has_upper)(up.wait_send)
    pl.when(has_lower)(down.wait_send)
    for q in everyone:
        swap[q].wait_send()
        for d in order:
            share(d, q).wait_send()


def fused(parts, cores, basis, blocks, col_index, send_rows, part_rows):
    width = basis.shape[1]
    lb = basis.shape[0] // BS
    halo = send_rows.shape[2]
    rows, stored = blocks.shape[1:3]
    full = 2 * width
    strips = width // BS
    ranks = 2 * parts
    piece = full // ranks
    bf16 = jnp.bfloat16
    dma = pltpu.SemaphoreType.DMA
    hbm = pl.BlockSpec(memory_space=pltpu.HBM)
    reduced = pl.pallas_call(
        functools.partial(kernel, parts, cores),
        out_shape=jax.ShapeDtypeStruct((piece, full), jnp.float32),
        in_specs=[hbm] * 5,
        out_specs=pl.BlockSpec(memory_space=pltpu.VMEM),
        scratch_shapes=[
            pltpu.SMEM((1,), jnp.int32),
            pltpu.SMEM((halo, 2), jnp.int32),
            pltpu.SMEM((rows, stored), jnp.int32),
            pltpu.VMEM((strips, lb, BS, BS), bf16),
            pltpu.VMEM((rows, stored, BS, BS), bf16),
            pltpu.VMEM((strips, lb, BS, BS), bf16),
            pltpu.VMEM((strips, lb + 2 * halo, BS, BS), bf16),
            pltpu.VMEM((strips, lb + 2 * halo, BS, BS), bf16),
            pltpu.VMEM((2, strips, halo, BS, BS), bf16),
            pltpu.VMEM((full, lb * BS), bf16),
            pltpu.VMEM((strips, rows * BS, BS), bf16),
            pltpu.VMEM((strips, lb * BS, BS), bf16),
            pltpu.VMEM((strips, full, BS), jnp.float32),
            pltpu.VMEM((strips, full, BS), bf16),
            pltpu.VMEM((strips, ranks - 1, piece, BS), bf16),
            dma((4 + strips,)),
            dma((4 + strips,)),
            dma((4 + strips,)),
            dma((2,)),
            dma((2,)),
            dma((strips, ranks - 1)),
            dma((strips, ranks - 1)),
            pltpu.SemaphoreType.REGULAR,
        ],
        compiler_params=pltpu.CompilerParams(
            collective_id=0, has_side_effects=True, vmem_limit_bytes=60 * 1024 * 1024
        ),
    )(part_rows, send_rows[0].T, col_index[0], basis.reshape(lb, BS, width), blocks[0])
    return reduced[None]


def solution(mesh):
    placed = (
        P(("grp", "mesh"), "col"),
        P("term", ("grp", "mesh", "col"), None, None, None),
        P("term", ("grp", "mesh", "col"), None),
        P(("grp", "mesh"), None, None),
        P(("grp", "mesh")),
    )
    parts, cols, cores = mesh.shape["mesh"], mesh.shape["col"], mesh.shape["term"]

    def local(basis, blocks, col_index, send_rows, part_rows):
        lb = basis.shape[0] // BS
        fits = (
            cols == 2
            and 2 <= parts <= 4
            and cores == 2
            and basis.shape[1] % BS == 0
            and lb % cores == 0
            and lb == 2 * blocks.shape[1]
            and (2 * basis.shape[1]) % (2 * parts * 16) == 0
        )
        if fits:
            return fused(parts, cores, basis, blocks, col_index, send_rows, part_rows)
        return general(basis, blocks, col_index, send_rows, part_rows)

    return jax.shard_map(
        local,
        mesh=mesh,
        in_specs=placed,
        out_specs=P("term", ("grp", "mesh", "col"), None),
        check_vma=False,
    )
```

```python
import functools

import jax
import jax.numpy as jnp
from jax import lax
from jax.experimental import pallas as pl
from jax.experimental.pallas import tpu as pltpu
from jax.sharding import PartitionSpec as P

BS = 128
MESH = pl.DeviceIdType.MESH


def from_behind(x, axis, by):
    length = lax.axis_size(axis)
    pairs = [(i, i + by) for i in range(length) if 0 <= i + by < length]
    return lax.ppermute(x, axis, pairs)


def general(basis, blocks, col_index, send_rows, part_rows):
    panel_width = basis.shape[1]
    local_blocks = basis.shape[0] // BS
    halo_count = send_rows.shape[2]
    device_blocks = blocks.shape[1]
    stored = blocks.shape[2]
    live = jnp.arange(local_blocks) < part_rows[0]
    panel = jnp.where(
        live[:, None, None],
        basis.reshape(local_blocks, BS, panel_width),
        jnp.zeros((), jnp.bfloat16),
    )
    going_down = jnp.take(panel, send_rows[0, 0], axis=0)
    going_up = jnp.take(panel, send_rows[0, 1], axis=0)
    from_lower = from_behind(going_up, "mesh", 1)
    from_upper = from_behind(going_down, "mesh", -1)
    ext_panel = jnp.concatenate([from_lower, panel, from_upper], axis=0)
    extended = lax.all_gather(ext_panel, "col", axis=2, tiled=True)
    full_width = extended.shape[2]
    term_blocks = blocks[0]
    slot_index = col_index[0]

    def accumulate(k, running):
        picked = jnp.take(extended, slot_index[:, k], axis=0)
        return running + jnp.einsum(
            "bij,bjc->bic", term_blocks[:, k], picked, preferred_element_type=jnp.float32
        )

    product = lax.fori_loop(
        0, stored, accumulate, jnp.zeros((device_blocks, BS, full_width), jnp.float32)
    )
    rounded = product.astype(jnp.bfloat16).reshape(device_blocks * BS, full_width)
    first_block = halo_count + lax.axis_index("col") * device_blocks
    own_rows = lax.dynamic_slice_in_dim(extended, first_block, device_blocks, 0).reshape(
        device_blocks * BS, full_width
    )
    reduced = lax.psum_scatter(
        lax.dot_general(
            own_rows, rounded, (((0,), (0,)), ((), ())), preferred_element_type=jnp.float32
        ),
        ("mesh", "col"),
        scatter_dimension=0,
        tiled=True,
    )
    return reduced[None]


def kernel(
    parts,
    cores,
    part_hbm,
    send_hbm,
    col_hbm,
    basis_ref,
    blocks_ref,
    out_ref,
    part_ref,
    send_ref,
    col_ref,
    basis_v,
    blocks_v,
    other_raw,
    ext_own,
    ext_other,
    stage,
    turned,
    p_send,
    p_all,
    g32,
    g_send,
    g_recv,
    local_sem,
    x_send,
    x_recv,
    z_send,
    z_recv,
    g_ssem,
    g_rsem,
    ok_sem,
):
    g = lax.axis_index("grp")
    m = lax.axis_index("mesh")
    c = lax.axis_index("col")
    t = lax.axis_index("term")
    strips, lb = basis_v.shape[:2]
    lane = basis_v.shape[3]
    width = strips * lane
    halo = send_ref.shape[0]
    rows, stored = blocks_v.shape[:2]
    ranks = 2 * parts
    rank = 2 * m + c
    half = lb // cores
    piece = g_send.shape[1] // ranks
    opposite = (g, m, 1 - c, t)
    sibling = (g, m, c, 1 - t)
    below = lax.rem(m + parts - 1, parts)
    above = lax.rem(m + 1, parts)
    has_lower = m > 0
    has_upper = m < parts - 1
    everyone = range(strips)

    def strip(q):
        return pl.ds(q * lane, lane)

    load_basis = [
        pltpu.make_async_copy(basis_ref.at[:, :, strip(q)], basis_v.at[q], local_sem.at[4 + q]) for q in everyone
    ]
    load_small = [
        pltpu.make_async_copy(hbm, ref, local_sem.at[1 + n])
        for n, (hbm, ref) in enumerate(((send_hbm, send_ref), (part_hbm, part_ref), (col_hbm, col_ref)))
    ]
    load_blocks = pltpu.make_async_copy(blocks_ref, blocks_v, local_sem.at[0])
    for load in load_basis + load_small + [load_blocks]:
        load.start()

    def peer(d):
        r = lax.rem(rank + d, ranks)
        return (g, r // 2, lax.rem(r, 2), t), r

    for load in load_basis + load_small:
        load.wait()
    for j in range(halo):
        for q in everyone:
            stage[0, q, j] = basis_v[q, send_ref[j, 1]]
            stage[1, q, j] = basis_v[q, send_ref[j, 0]]

    barrier = pltpu.get_barrier_semaphore()
    for to in (sibling, opposite):
        pl.semaphore_signal(barrier, inc=1, device_id=to, device_id_type=MESH)
    for there, z in ((has_lower, below), (has_upper, above)):

        @pl.when(there)
        def _():
            for side in (c, 1 - c):
                pl.semaphore_signal(barrier, inc=1, device_id=(g, z, side, t), device_id_type=MESH)

    sides = has_lower.astype(jnp.int32) + has_upper.astype(jnp.int32)
    pl.semaphore_wait(barrier, 2 + 2 * sides)

    def remote(src, dst, ssem, rsem, to):
        return pltpu.make_async_remote_copy(
            src_ref=src, dst_ref=dst, send_sem=ssem, recv_sem=rsem, device_id=to, device_id_type=MESH
        )

    span = pl.ds(t * half, half)
    edge = pl.ds(t * (lb + halo), halo)
    ahead, behind = m + 1 - 2 * t, m - 1 + 2 * t
    has_ahead = jnp.logical_and(ahead >= 0, ahead < parts)
    has_behind = jnp.logical_and(behind >= 0, behind < parts)
    forward = lax.rem(ahead + parts, parts)
    across = remote(basis_v.at[:, span], other_raw.at[:, span], x_send.at[0], x_recv.at[0], opposite)
    inner = remote(other_raw.at[:, span], other_raw.at[:, span], x_send.at[1], x_recv.at[1], sibling)
    slant = remote(stage.at[t], ext_other.at[:, edge], x_send.at[2], x_recv.at[2], (g, forward, 1 - c, t))
    inner_edge = remote(ext_other.at[:, edge], ext_other.at[:, edge], x_send.at[3], x_recv.at[3], sibling)
    placed = pl.ds(c * rows * BS, rows * BS)
    swap = [remote(p_send.at[q], p_all.at[q, placed], x_send.at[4 + q], x_recv.at[4 + q], opposite) for q in everyone]
    low = pl.ds(0, halo)
    high = pl.ds(lb + halo, halo)
    up = remote(stage.at[0], ext_own.at[:, low], z_send.at[0], z_recv.at[0], (g, above, c, t))
    down = remote(stage.at[1], ext_own.at[:, high], z_send.at[1], z_recv.at[1], (g, below, c, t))

    across.start()
    pl.when(has_upper)(up.start)
    pl.when(has_lower)(down.start)
    pl.when(has_ahead)(slant.start)

    def fill(raw, ext):
        for q in everyone:
            for i in range(lb):
                ext[q, halo + i] = jnp.where(i < part_ref[0], raw[q, i], jnp.zeros((), jnp.bfloat16))

    blank = jnp.zeros((strips, halo, BS, lane), jnp.bfloat16)
    for there, where in ((has_lower, low), (has_upper, high)):

        @pl.when(jnp.logical_not(there))
        def _():
            ext_own[:, where] = blank
            ext_other[:, where] = blank

    def product(ext, r):
        total = jnp.zeros((BS, width), jnp.float32)
        step = 2 if stored % 2 == 0 else 1
        for k in range(0, stored, step):
            left = jnp.concatenate([blocks_v[r, k + j] for j in range(step)], axis=1)
            right = jnp.concatenate(
                [
                    jnp.concatenate([ext[q, col_ref[r, k + j]] for q in everyone], axis=1)
                    for j in range(step)
                ],
                axis=0,
            )
            total = total + jnp.dot(left, right, preferred_element_type=jnp.float32)
        return total.astype(jnp.bfloat16)

    def turn(ext, where):
        for q in everyone:
            body = ext[q, pl.ds(halo, lb)].reshape(lb * BS, lane)
            turned[pl.ds(where * width + q * lane, lane)] = body.T

    def share(d, q):
        to, r = peer(d)
        return remote(
            g_send.at[q, pl.ds(r * piece, piece)],
            g_recv.at[q, d - 1],
            g_ssem.at[q, d - 1],
            g_rsem.at[q, d - 1],
            to,
        )

    order = sorted(range(1, ranks), key=lambda d: abs(d - parts))

    fill(basis_v, ext_own)
    load_blocks.wait()
    pl.when(has_lower)(up.wait_recv)
    pl.when(has_upper)(down.wait_recv)
    for there, z in ((has_lower, below), (has_upper, above)):

        @pl.when(there)
        def _():
            pl.semaphore_signal(ok_sem, inc=1, device_id=(g, z, c, t), device_id_type=MESH)

    for r in range(rows):
        value = product(ext_own, r)
        for q in everyone:
            p_send[q, pl.ds(r * BS, BS)] = value[:, q * lane : (q + 1) * lane]
    for q in everyone:
        swap[q].start()
    across.wait_recv()
    inner.start()

    @pl.when(has_behind)
    def _():
        slant.wait_recv()
        inner_edge.start()

    turn(ext_own, c)
    inner.wait_recv()
    fill(other_raw, ext_other)
    turn(ext_other, 1 - c)
    pl.when(has_ahead)(inner_edge.wait_recv)
    for r in range(rows):
        value = product(ext_other, r)
        for q in everyone:
            p_all[q, pl.ds(c * rows * BS + r * BS, BS)] = value[:, q * lane : (q + 1) * lane]
    pl.semaphore_wait(ok_sem, sides)

    for q in everyone:
        swap[q].wait_recv()
        value = jnp.dot(turned[...], p_all[q], preferred_element_type=jnp.float32)
        g32[q] = value
        g_send[q] = value.astype(jnp.bfloat16)
        for d in order:
            share(d, q).start()

    for q in everyone:
        same = g32[q, pl.ds(rank * piece, piece)]
        crossed = jnp.zeros_like(same)
        for d in reversed(order):
            share(d, q).wait_recv()
            if d % 2:
                crossed = crossed + g_recv[q, d - 1].astype(jnp.float32)
            else:
                same = same + g_recv[q, d - 1].astype(jnp.float32)
        out_ref[:, pl.ds(pl.multiple_of((1 - c) * width + q * lane, lane), lane)] = same
        out_ref[:, pl.ds(pl.multiple_of(c * width + q * lane, lane), lane)] = crossed

    across.wait_send()
    inner.wait_send()
    pl.when(has_ahead)(slant.wait_send)
    pl.when(has_behind)(inner_edge.wait_send)
    pl.when(has_upper)(up.wait_send)
    pl.when(has_lower)(down.wait_send)
    for q in everyone:
        swap[q].wait_send()
        for d in order:
            share(d, q).wait_send()


def fused(parts, cores, basis, blocks, col_index, send_rows, part_rows):
    width = basis.shape[1]
    lb = basis.shape[0] // BS
    halo = send_rows.shape[2]
    rows, stored = blocks.shape[1:3]
    full = 2 * width
    strips = 1
    lane = width // strips
    ranks = 2 * parts
    piece = full // ranks
    bf16 = jnp.bfloat16
    dma = pltpu.SemaphoreType.DMA
    hbm = pl.BlockSpec(memory_space=pltpu.HBM)
    reduced = pl.pallas_call(
        functools.partial(kernel, parts, cores),
        out_shape=jax.ShapeDtypeStruct((piece, full), jnp.float32),
        in_specs=[hbm] * 5,
        out_specs=pl.BlockSpec(memory_space=pltpu.VMEM),
        scratch_shapes=[
            pltpu.SMEM((1,), jnp.int32),
            pltpu.SMEM((halo, 2), jnp.int32),
            pltpu.SMEM((rows, stored), jnp.int32),
            pltpu.VMEM((strips, lb, BS, lane), bf16),
            pltpu.VMEM((rows, stored, BS, BS), bf16),
            pltpu.VMEM((strips, lb, BS, lane), bf16),
            pltpu.VMEM((strips, lb + 2 * halo, BS, lane), bf16),
            pltpu.VMEM((strips, lb + 2 * halo, BS, lane), bf16),
            pltpu.VMEM((2, strips, halo, BS, lane), bf16),
            pltpu.VMEM((full, lb * BS), bf16),
            pltpu.VMEM((strips, rows * BS, lane), bf16),
            pltpu.VMEM((strips, lb * BS, lane), bf16),
            pltpu.VMEM((strips, full, lane), jnp.float32),
            pltpu.VMEM((strips, full, lane), bf16),
            pltpu.VMEM((strips, ranks - 1, piece, lane), bf16),
            dma((4 + strips,)),
            dma((4 + strips,)),
            dma((4 + strips,)),
            dma((2,)),
            dma((2,)),
            dma((strips, ranks - 1)),
            dma((strips, ranks - 1)),
            pltpu.SemaphoreType.REGULAR,
        ],
        compiler_params=pltpu.CompilerParams(
            collective_id=0, has_side_effects=True, vmem_limit_bytes=60 * 1024 * 1024
        ),
    )(part_rows, send_rows[0].T, col_index[0], basis.reshape(lb, BS, width), blocks[0])
    return reduced[None]


def solution(mesh):
    placed = (
        P(("grp", "mesh"), "col"),
        P("term", ("grp", "mesh", "col"), None, None, None),
        P("term", ("grp", "mesh", "col"), None),
        P(("grp", "mesh"), None, None),
        P(("grp", "mesh")),
    )
    parts, cols, cores = mesh.shape["mesh"], mesh.shape["col"], mesh.shape["term"]

    def local(basis, blocks, col_index, send_rows, part_rows):
        lb = basis.shape[0] // BS
        fits = (
            cols == 2
            and 2 <= parts <= 4
            and cores == 2
            and basis.shape[1] % BS == 0
            and lb % cores == 0
            and lb == 2 * blocks.shape[1]
            and (2 * basis.shape[1]) % (2 * parts * 16) == 0
        )
        if fits:
            return fused(parts, cores, basis, blocks, col_index, send_rows, part_rows)
        return general(basis, blocks, col_index, send_rows, part_rows)

    return jax.shard_map(
        local,
        mesh=mesh,
        in_specs=placed,
        out_specs=P("term", ("grp", "mesh", "col"), None),
        check_vma=False,
    )
```
